32 devices in a mesh: dp: 4 (over y, x), seq: 8 (over z, core).
Axes of the slice: x: 2, y: 2, z: 4, core: 2. Of those that a mesh axis runs over, the one named last changes fastest.
Arguments:
- inputs: bfloat16 [4096, 6144], P('seq'), may hold values from -6 to 6
- qkv_weight: bfloat16 [6144, 12288], P(None, ('dp', 'seq')), may hold values from -0.078125 to 0.078125
- log_decay: float32 [32, 4096], P('dp', 'seq'), may hold values from -1 to 0, as said below
- out_gain: float32 [32, 128], P('dp'), may hold values from 0.1 to 1.9
Outputs:
- attended: bfloat16 [4096, 4096], P('seq', 'dp')
The draws below stay inside these ranges and needn't reach their ends.
Inputs may be any that keep to these rules, and one draw needn't show every extreme that they name: `log_decay`: log of a decay factor, negative at every position.
All inputs are finite; a program needn't handle non-finite values.
Results may differ from the reference program's by a relative error of at most 0.0055.
Values may be sent and summed in bfloat16 or wider, within the bound.
A program may use at most 128 MiB of HBM per device.

```python
import jax
import jax.numpy as jnp
from jax import lax

D = 6144
HD = 128
WINDOW_HEADS = 32
TOK_DEV = 512
SEQ_LEN = 4096
QKV = 12288


def draw_inputs(key, part):
    key_list = jax.random.split(key, 2)
    stretch_count = (SEQ_LEN + 127) // 128
    log_scale = jax.random.uniform(key_list[0], (stretch_count, 1), jnp.float32, -2.3, 0.4)
    row_scale = jnp.repeat(jnp.exp(log_scale), 128, axis=0)[:SEQ_LEN]
    standard = jax.random.normal(key_list[1], (SEQ_LEN, D), jnp.float32)
    return jnp.clip(standard * row_scale, -6.0, 6.0).astype(jnp.bfloat16)


def draw_log_decay(key, part):
    every_key_row = jax.random.split(key, 7)
    fast_share = 0.5
    fast_heads = jax.random.uniform(every_key_row[0], (WINDOW_HEADS, 1)) < fast_share
    fast_rate = jnp.exp(jax.random.uniform(every_key_row[1], (WINDOW_HEADS, 1), jnp.float32, jnp.log(1.0 / 50.0), jnp.log(1.0 / 30.0)))
    gradual_rate = jnp.exp(jax.random.uniform(every_key_row[2], (WINDOW_HEADS, 1), jnp.float32, jnp.log(0.05), jnp.log(0.5))) / SEQ_LEN
    default_decay_rate = jnp.where(fast_heads, fast_rate, gradual_rate)
    position_decay_factor = jax.random.uniform(every_key_row[3], (WINDOW_HEADS, SEQ_LEN), jnp.float32, 0.5, 1.5)
    block_decay_factor = jax.random.uniform(every_key_row[4], (WINDOW_HEADS, SEQ_LEN // TOK_DEV), jnp.float32, 0.5, 1.0)
    block_decay_factor = jnp.repeat(block_decay_factor, TOK_DEV, axis=1)
    places = jax.random.randint(every_key_row[5], (WINDOW_HEADS, 2), 0, SEQ_LEN)
    spike_height = jax.random.uniform(every_key_row[6], (WINDOW_HEADS, 2), jnp.float32, 0.22, 0.5)
    positions = jnp.arange(SEQ_LEN)
    agreement_count = (positions[None, :, None] == places[:, None, :]).astype(jnp.float32)
    spike_total_sum = jnp.sum(agreement_count * spike_height[:, None, :], axis=-1)
    return -(default_decay_rate * position_decay_factor * block_decay_factor + spike_total_sum)


def steps_of(own_key, extent, shards, least, top_value):
    def one(dim, shards_of):
        draws = jax.random.uniform(jax.random.fold_in(jax.random.fold_in(own_key, 6), dim), (shards_of,), jnp.float32, least / len(shards), top_value / len(shards))
        return jnp.repeat(jnp.exp(draws), extent[dim] // shards_of).reshape((-1,) + (1,) * (len(extent) - dim - 1))

    loudness = one(*shards[0])
    for cut in shards[1:]:
        loudness = loudness * one(*cut)
    return loudness


def gaussian(key, extent, scale, reach, shards=(), held_as=jnp.bfloat16):
    gain = steps_of(key, extent, shards, -0.22, 0.18) if shards else 1.0
    array = jax.random.normal(key, extent, jnp.float32) * scale * gain
    return jnp.minimum(jnp.maximum(array, -reach), reach).astype(held_as)


def setup_inputs(seed: int = 0) -> dict:
    seeds = jax.random.split(jax.random.key(seed), 5)
    inputs = draw_inputs(jax.random.fold_in(seeds[4], 71), 0)
    qkv_weight = gaussian(seeds[1], (D, QKV), D ** -0.5, 0.078125, ((1, 32),))
    log_decay = draw_log_decay(jax.random.fold_in(seeds[4], 71), 0)
    out_gain = jnp.clip(1.0 + 0.18 * jax.random.normal(seeds[3], (WINDOW_HEADS, HD), jnp.float32), 0.1, 1.9)
    return dict(inputs=inputs, qkv_weight=qkv_weight, log_decay=log_decay, out_gain=out_gain)


def block_terms(queries, keys, values, block_decay):
    cumulated = jnp.cumsum(block_decay, axis=-1)
    tok_count = queries.shape[-2]
    row_index = jnp.arange(tok_count)[:, None]
    col_index = jnp.arange(tok_count)[None, :]
    causal = row_index >= col_index
    spread = cumulated[:, :, None] - cumulated[:, None, :]
    decay_mask = jnp.where(causal, jnp.exp(jnp.where(causal, spread, 0.0)), 0.0)
    scores = jnp.einsum('htd,hsd->hts', queries.astype(jnp.float32), keys.astype(jnp.float32))
    weights = (scores * decay_mask).astype(jnp.bfloat16)
    intra_term = jnp.einsum('hts,hsd->htd', weights.astype(jnp.float32), values.astype(jnp.float32))
    tail_decay = jnp.exp(cumulated[:, -1:] - cumulated)
    keys_decayed = keys.astype(jnp.float32) * tail_decay[:, :, None]
    update = jnp.einsum('hsd,hse->hde', keys_decayed, values.astype(jnp.float32), precision=lax.Precision.HIGHEST)
    block_total = cumulated[:, -1]
    queries_decayed = queries.astype(jnp.float32) * jnp.exp(cumulated)[:, :, None]
    return (intra_term, update, block_total, queries_decayed)

def finish_heads(intra_term, queries_decayed, carried, out_gain):
    outer_term = jnp.einsum('htd,hde->hte', queries_decayed, carried, precision=lax.Precision.HIGHEST)
    combined = intra_term + outer_term
    root_mean = lax.rsqrt(lax.optimization_barrier(jnp.mean(combined * combined, axis=-1, keepdims=True)) + 1e-05)
    return combined * root_mean * out_gain[:, None, :]

def reference(inputs, qkv_weight, log_decay, out_gain):
    block_count = SEQ_LEN // TOK_DEV
    blocks_in = inputs.reshape(block_count, TOK_DEV, D)
    blocks_decay = jnp.transpose(log_decay.reshape(WINDOW_HEADS, block_count, TOK_DEV), (1, 0, 2))

    def advance(carried, block_item):
        block_in, block_decay = block_item
        projected = jnp.dot(block_in, qkv_weight, preferred_element_type=jnp.float32)
        activated = jax.nn.silu(projected).astype(jnp.bfloat16).reshape(TOK_DEV, WINDOW_HEADS, 3, HD)
        activated = jnp.transpose(activated, (2, 1, 0, 3))
        intra_term, update, block_total, queries_decayed = block_terms(activated[0], activated[1], activated[2], block_decay)
        normed = finish_heads(intra_term, queries_decayed, carried, out_gain)
        renewed = jnp.exp(block_total)[:, None, None] * carried + update
        result = jnp.transpose(normed, (1, 0, 2)).reshape(TOK_DEV, WINDOW_HEADS * HD).astype(jnp.bfloat16)
        return (renewed, result)
    start_state = jnp.zeros((WINDOW_HEADS, HD, HD), jnp.float32)
    _, results = lax.scan(advance, start_state, (blocks_in, blocks_decay))
    return results.reshape(SEQ_LEN, WINDOW_HEADS * HD)
```

```python
import functools

import jax
import jax.numpy as jnp
from jax import lax
from jax.experimental import pallas as pl
from jax.experimental.pallas import tpu as pltpu
from jax.sharding import PartitionSpec as P

MESH = pl.DeviceIdType.MESH
SUBS = 4


def prefix_2(value, axis, join, neutral):
    count, mine = (lax.axis_size(axis), lax.axis_index(axis))
    pieces = jax.tree.map(lambda part: lax.all_gather(part, axis), value)
    subtotal = jax.tree.map(
        lambda part, zero: jnp.full_like(part, 0) + jnp.asarray(zero, part.dtype), value, neutral
    )

    def turn(position, subtotal):
        longer = join(subtotal, jax.tree.map(lambda part: part[position], pieces))
        return jax.tree.map(lambda new, old: jnp.where(position < mine, new, old), longer, subtotal)

    return lax.fori_loop(0, count - 1, turn, subtotal)


def running(decays):
    index = jnp.arange(decays.shape[-1])
    upto = (index[:, None] <= index[None, :]).astype(jnp.float32)
    return jnp.dot(decays, upto, precision=lax.Precision.HIGHEST)


def block_terms(queries, keys, values, cumulated):
    tok_count = queries.shape[-2]
    row_index = jnp.arange(tok_count)[:, None]
    col_index = jnp.arange(tok_count)[None, :]
    causal = row_index >= col_index
    spread = cumulated[:, :, None] - cumulated[:, None, :]
    decay_mask = jnp.where(causal, jnp.exp(jnp.where(causal, spread, 0.0)), 0.0)
    scores = jnp.einsum("htd,hsd->hts", queries, keys, preferred_element_type=jnp.float32)
    weights = (scores * decay_mask).astype(jnp.bfloat16)
    intra_term = jnp.einsum("hts,hsd->htd", weights, values, preferred_element_type=jnp.float32)
    tail_decay = jnp.exp(cumulated[:, -1:] - cumulated)
    keys_decayed = keys.astype(jnp.float32) * tail_decay[:, :, None]
    update = jnp.einsum(
        "hsd,hse->hde", keys_decayed, values.astype(jnp.float32), precision=lax.Precision.HIGHEST
    )
    block_total = cumulated[:, -1]
    queries_decayed = queries.astype(jnp.float32) * jnp.exp(cumulated)[:, :, None]
    return (intra_term, update, block_total, queries_decayed)


def finish_heads(intra_term, queries_decayed, carried, gains):
    outer_term = jnp.einsum(
        "htd,hde->hte", queries_decayed, carried, precision=lax.Precision.HIGHEST
    )
    combined = intra_term + outer_term
    root_mean = lax.rsqrt(jnp.mean(combined * combined, axis=-1, keepdims=True) + 1e-05)
    return combined * root_mean * gains[:, None, :]


def chain_combine(earlier_pair, later_pair):
    return (
        earlier_pair[0] + later_pair[0],
        jnp.exp(later_pair[0])[:, None, None] * earlier_pair[1] + later_pair[1],
    )


def shards_wide(inputs, qkv_weight, log_decay, out_gain):
    tok_count = inputs.shape[0]
    local_heads = out_gain.shape[0]
    head_size = out_gain.shape[1]
    projected = jnp.dot(
        inputs,
        lax.all_gather(qkv_weight, "seq", axis=1, tiled=True),
        preferred_element_type=jnp.float32,
    )
    activated = jax.nn.silu(projected).astype(jnp.bfloat16)
    grouped = jnp.transpose(activated.reshape(tok_count, local_heads, 3, head_size), (2, 1, 0, 3))
    intra_term, update, block_total, queries_decayed = block_terms(
        grouped[0], grouped[1], grouped[2], running(log_decay)
    )
    identity = (jnp.zeros_like(block_total), jnp.zeros_like(update))
    prefix = prefix_2((block_total, update), "seq", chain_combine, identity)
    normed = finish_heads(intra_term, queries_decayed, prefix[1], out_gain)
    return (
        jnp.transpose(normed, (1, 0, 2))
        .reshape(tok_count, local_heads * head_size)
        .astype(jnp.bfloat16)
    )


def place():
    dp, seq = lax.axis_index("dp"), lax.axis_index("seq")
    return dp, seq, dp // 2, dp % 2, seq // 2, seq % 2


def gather_kernel(
    line, x_ref, w_ref, out, xg, wg, total,
    own_send, own_recv, first_send, z_send, z_recv, y_send, y_recv,
    wx_send, wx_recv, wf_send, wf_recv, wp_send, wp_recv, local_sem,
):
    dp, seq, y, x, z, c = place()
    rows = x_ref.shape[0] // 2
    half = rows // 2
    sub = half // SUBS
    width = w_ref.shape[1]
    pieces = (line - 1) * SUBS
    depth = w_ref.shape[0] // pieces
    x_pair = {"dp": dp + 1 - 2 * x, "seq": seq}
    y_pair = {"dp": dp + 2 - 4 * y, "seq": seq}
    c_pair = {"dp": dp, "seq": seq + 1 - 2 * c}

    def at(position, core):
        return {"dp": dp, "seq": 2 * position + core}

    barrier = pltpu.get_barrier_semaphore()
    for target in (x_pair, y_pair, c_pair):
        pl.semaphore_signal(barrier, inc=1, device_id=target, device_id_type=MESH)
    for step in (1, -1):
        @pl.when((z + step >= 0) & (z + step < line))
        def _():
            for core in (0, 1):
                pl.semaphore_signal(barrier, inc=1, device_id=at(z + step, core), device_id_type=MESH)
    count = 3 + 2 * ((z > 0).astype(jnp.int32) + (z < line - 1).astype(jnp.int32))
    pl.semaphore_wait(barrier, count)

    def remote(src, dst, send, recv, target):
        return pltpu.make_async_remote_copy(
            src_ref=src, dst_ref=dst, send_sem=send, recv_sem=recv,
            device_id=target, device_id_type=MESH,
        )

    def strip(position, side, r):
        return xg.at[position, pl.ds(pl.multiple_of(side * half + r * sub, sub), sub)]

    def first(core, step, r):
        start = pl.multiple_of(core * rows + y * half + r * sub, sub)
        return remote(
            x_ref.at[pl.ds(start, sub)], strip(z, y, r),
            first_send.at[core, (step + 1) // 2, r], z_recv.at[z, r], at(z + step, core),
        )

    def columns(xx, cc):
        return pl.ds(pl.multiple_of((xx * 2 + cc) * width, 128), width)

    def weight_first(j):
        part = pl.ds(j * depth, depth)
        return remote(
            w_ref.at[part], wg.at[part, columns(x, c)], wx_send.at[j], wx_recv.at[j], x_pair
        )

    def weight_next(j):
        part = wg.at[pl.ds(j * depth, depth), columns(1 - x, c)]
        return remote(part, part, wf_send.at[j], wf_recv.at[j], c_pair)

    def own_rows(core):
        return x_ref.at[pl.ds(pl.multiple_of(core * rows, rows), rows)]

    own_local = pltpu.make_async_copy(own_rows(c), xg.at[z], local_sem.at[0])
    own_peer = remote(own_rows(1 - c), xg.at[z], own_send, own_recv, c_pair)
    w_local = pltpu.make_async_copy(w_ref, wg.at[:, columns(x, c)], local_sem.at[1])
    w_peer = remote(w_ref, wg.at[:, columns(x, c)], wp_send, wp_recv, c_pair)

    def exists(position):
        return (position >= 0) & (position < line)

    for r in range(SUBS):
        for step in (1, -1):
            @pl.when((c == x) & exists(z + step))
            def _():
                for core in (0, 1):
                    first(core, step, r).start()
    for j in range(pieces):
        weight_first(j).start()

    @pl.when(c == x)
    def _():
        own_local.start()
        own_peer.start()
    w_peer.start()
    w_local.start()

    def z_next(origin, step, r):
        part = strip(origin, y, r)
        return remote(part, part, z_send.at[origin, r], z_recv.at[origin, r], at(z - step, c))

    def y_next(origin, side, r):
        part = strip(origin, side, r)
        return remote(part, part, y_send.at[origin, r], y_recv.at[origin, r], y_pair)

    model = w_ref.shape[0]
    early = (line - 2) * SUBS * depth
    tile = 2 * out.shape[4]

    def project(position, xx, low, high, begin=False, resume=False):
        def turn(n, carry):
            start = pl.multiple_of(n * tile, 128)
            cols = pl.ds(pl.multiple_of(xx * 2 * width + n * tile, 128), tile)
            term = jnp.dot(
                xg[position, :, low:high], wg[low:high, cols], preferred_element_type=jnp.float32
            )
            if begin:
                total[position, :, pl.ds(start, tile)] = term
                return carry
            if resume:
                term = term + total[position, :, pl.ds(start, tile)]
            term = (term * jax.nn.sigmoid(term)).astype(out.dtype)
            for i in (0, 1):
                j = 2 * n + i
                out[j % 3, position, 2 * xx + j // 3] = term[:, i * tile // 2 : (i + 1) * tile // 2]
            return carry

        lax.fori_loop(0, 2 * width // tile, turn, 0)

    def around(k, act):
        for step in (1, -1):
            @pl.when(exists(z + step * k))
            def _():
                act(z + step * k)

    def y_wait(k):
        def act(origin):
            for r in range(SUBS):
                y_next(origin, 1 - y, r).wait_recv()

        around(k, act)

    @pl.when(c == x)
    def _():
        own_local.wait()

    @pl.when(c != x)
    def _():
        own_peer.wait_recv()

    w_local.wait()
    w_peer.wait()
    project(z, x, 0, model)

    for k in range(1, line):
        for r in range(SUBS):
            for step in (1, -1):
                origin = z + step * k

                @pl.when(exists(origin))
                def _():
                    z_next(origin, step, r).wait_recv()
                    y_next(origin, y, r).start()

                    @pl.when(exists(z - step))
                    def _():
                        z_next(origin, step, r).start()
            j = (k - 1) * SUBS + r
            weight_first(j).wait_recv()
            weight_next(j).start()
            if k >= 2 and r == 1:
                y_wait(k - 1)
                around(k - 1, lambda origin: project(origin, x, 0, model))
                if k == line - 1:
                    around(k - 1, lambda origin: project(origin, 1 - x, 0, early, begin=True))
        if k == line - 2:
            for j in range((line - 2) * SUBS):
                weight_next(j).wait_recv()
            project(z, 1 - x, 0, early, begin=True)
            for before in range(1, k):
                around(before, lambda origin: project(origin, 1 - x, 0, early, begin=True))

    for j in range((line - 2) * SUBS, pieces):
        weight_next(j).wait_recv()
    project(z, 1 - x, early, model, resume=True)
    for k in range(1, line - 1):
        around(k, lambda origin: project(origin, 1 - x, early, model, resume=True))
    y_wait(line - 1)
    around(line - 1, lambda origin: project(origin, x, 0, model))
    around(line - 1, lambda origin: project(origin, 1 - x, 0, model))

    for k in range(1, line):
        for r in range(SUBS):
            for step in (1, -1):
                origin = z + step * k

                @pl.when(exists(origin))
                def _():
                    y_next(origin, y, r).wait_send()

                    @pl.when(exists(z - step))
                    def _():
                        z_next(origin, step, r).wait_send()
            j = (k - 1) * SUBS + r
            weight_first(j).wait_send()
            weight_next(j).wait_send()
    for r in range(SUBS):
        for step in (1, -1):
            @pl.when((c == x) & exists(z + step))
            def _():
                for core in (0, 1):
                    first(core, step, r).wait_send()

    @pl.when(c == x)
    def _():
        own_peer.wait_send()


def gather(line, inputs, weight, head_size):
    tok, depth = inputs.shape
    dma = pltpu.SemaphoreType.DMA
    pieces = (line - 1) * SUBS
    width = weight.shape[1]
    any_space = pl.BlockSpec(memory_space=pl.ANY)
    return pl.pallas_call(
        functools.partial(gather_kernel, line),
        out_shape=jax.ShapeDtypeStruct((3, line, 4, tok // 2, head_size), inputs.dtype),
        in_specs=[any_space] * 2,
        out_specs=pl.BlockSpec(memory_space=pltpu.VMEM),
        scratch_shapes=[
            pltpu.VMEM((line, tok // 2, depth), inputs.dtype),
            pltpu.VMEM((depth, 4 * width), weight.dtype),
            pltpu.VMEM((line, tok // 2, 2 * width), jnp.float32),
            dma, dma, dma((2, 2, SUBS)), dma((line, SUBS)), dma((line, SUBS)),
            dma((line, SUBS)), dma((line, SUBS)),
            dma((pieces,)), dma((pieces,)), dma((pieces,)), dma((pieces,)),
            dma, dma, dma((2,)),
        ],
        compiler_params=pltpu.CompilerParams(
            collective_id=0, has_side_effects=True, vmem_limit_bytes=50 << 20
        ),
        name="gather",
    )(inputs, weight)


def share_kernel(l_ref, g_ref, ld, gd, l_send, l_recv, g_send, g_recv, local_sem):
    dp, seq, y, x, z, c = place()
    seqs = ld.shape[1]

    def device(xx, ss):
        return {"dp": 2 * y + xx, "seq": ss}

    def others(act):
        for xx in (0, 1):
            for ss in range(seqs):
                @pl.when((xx != x) | (ss != seq))
                def _():
                    act(xx, ss)

    barrier = pltpu.get_barrier_semaphore()
    others(
        lambda xx, ss: pl.semaphore_signal(
            barrier, inc=1, device_id=device(xx, ss), device_id_type=MESH
        )
    )
    pl.semaphore_wait(barrier, 2 * seqs - 1)

    def push(xx, ss):
        return pltpu.make_async_remote_copy(
            src_ref=l_ref, dst_ref=ld.at[x, seq],
            send_sem=l_send.at[xx, ss], recv_sem=l_recv.at[x, seq],
            device_id=device(xx, ss), device_id_type=MESH,
        )

    def pull(xx, ss):
        return pltpu.make_async_remote_copy(
            src_ref=l_ref, dst_ref=ld.at[xx, ss],
            send_sem=l_send.at[xx, ss], recv_sem=l_recv.at[xx, ss],
            device_id=device(xx, ss), device_id_type=MESH,
        )

    gain = pltpu.make_async_remote_copy(
        src_ref=g_ref, dst_ref=gd.at[x], send_sem=g_send, recv_sem=g_recv,
        device_id=device(1 - x, seq), device_id_type=MESH,
    )
    l_local = pltpu.make_async_copy(l_ref, ld.at[x, seq], local_sem.at[0])
    g_local = pltpu.make_async_copy(g_ref, gd.at[x], local_sem.at[1])
    others(lambda xx, ss: push(xx, ss).start())
    gain.start()
    l_local.start()
    g_local.start()
    others(lambda xx, ss: pull(xx, ss).wait_recv())
    others(lambda xx, ss: push(xx, ss).wait_send())
    gain.wait()
    l_local.wait()
    g_local.wait()


def share(seqs, log_decay, out_gain):
    dma = pltpu.SemaphoreType.DMA
    vmem = pl.BlockSpec(memory_space=pltpu.VMEM)
    return pl.pallas_call(
        share_kernel,
        out_shape=(
            jax.ShapeDtypeStruct((2, seqs) + log_decay.shape, log_decay.dtype),
            jax.ShapeDtypeStruct((2,) + out_gain.shape, out_gain.dtype),
        ),
        in_specs=[vmem] * 2,
        out_specs=(vmem, vmem),
        scratch_shapes=[dma((2, seqs)), dma((2, seqs)), dma, dma, dma((2,))],
        compiler_params=pltpu.CompilerParams(
            collective_id=2, has_side_effects=True, vmem_limit_bytes=4 << 20
        ),
        name="share",
    )(log_decay, out_gain)


def scatter_kernel(line, tiles, out, send_sem, recv_sem, local_sem):
    dp, seq, y, x, z, c = place()
    rows, cols = tiles.shape[2], tiles.shape[3]

    def device(xx, zz, cc):
        return {"dp": 2 * y + xx, "seq": 2 * zz + cc}

    barrier = pltpu.get_barrier_semaphore()
    for zz in range(line):
        for cc in (0, 1):
            @pl.when((zz != z) | (cc != c) | (c != x))
            def _():
                pl.semaphore_signal(
                    barrier, inc=1, device_id=device(c, zz, cc), device_id_type=MESH
                )
    pl.semaphore_wait(barrier, 2 * line - (c == x).astype(jnp.int32))

    def area(zz, cc):
        return out.at[
            pl.ds(pl.multiple_of(cc * rows, rows), rows),
            pl.ds(pl.multiple_of(zz * cols, 128), cols),
        ]

    def push(zz, xx):
        return pltpu.make_async_remote_copy(
            src_ref=tiles.at[zz, xx], dst_ref=area(z, c),
            send_sem=send_sem.at[zz, xx], recv_sem=recv_sem.at[z, c],
            device_id=device(xx, zz, x), device_id_type=MESH,
        )

    def pull(zz, cc):
        return pltpu.make_async_remote_copy(
            src_ref=tiles.at[0, 0], dst_ref=area(zz, cc),
            send_sem=send_sem.at[0, 0], recv_sem=recv_sem.at[zz, cc],
            device_id=device(1 - x, z, c), device_id_type=MESH,
        )

    local = pltpu.make_async_copy(tiles.at[z, x], area(z, c), local_sem)
    own = c == x
    for zz in range(line):
        for xx in (0, 1):
            @pl.when((zz != z) | (xx != x) | jnp.logical_not(own))
            def _():
                push(zz, xx).start()

    @pl.when(own)
    def _():
        local.start()
    for zz in range(line):
        for cc in (0, 1):
            @pl.when((zz != z) | (cc != c) | jnp.logical_not(own))
            def _():
                pull(zz, cc).wait_recv()
    for zz in range(line):
        for xx in (0, 1):
            @pl.when((zz != z) | (xx != x) | jnp.logical_not(own))
            def _():
                push(zz, xx).wait_send()

    @pl.when(own)
    def _():
        local.wait()


def scatter(line, tiles):
    dma = pltpu.SemaphoreType.DMA
    _, _, rows, cols = tiles.shape
    any_space = pl.BlockSpec(memory_space=pl.ANY)
    return pl.pallas_call(
        functools.partial(scatter_kernel, line),
        out_shape=jax.ShapeDtypeStruct((2 * rows, line * cols), tiles.dtype),
        in_specs=[any_space],
        out_specs=any_space,
        scratch_shapes=[dma((line, 2)), dma((line, 2)), dma],
        compiler_params=pltpu.CompilerParams(
            collective_id=1, has_side_effects=True, vmem_limit_bytes=1 << 20
        ),
        name="scatter",
    )(tiles)


def shards_quarter(inputs, qkv_weight, log_decay, out_gain):
    dps, seqs = lax.axis_size("dp"), lax.axis_size("seq")
    dp, seq, y, x, z, c = place()
    line = seqs // 2
    tok = inputs.shape[0]
    chunk = tok // 2
    local_heads, head_size = out_gain.shape
    heads = 4
    decays, gains = share(seqs, log_decay, out_gain)
    decays = lax.dynamic_slice_in_dim(decays, 2 * z, 2, axis=2)
    decays = jnp.transpose(decays, (1, 0, 2, 3)).reshape(line, 2, 2, 2, 2, chunk)
    decays = jnp.transpose(decays, (0, 1, 4, 2, 3, 5)).reshape(line, 2, 2, heads, chunk)
    gains = lax.dynamic_slice_in_dim(gains, 2 * z, 2, axis=1).reshape(heads, head_size)
    totals = jnp.sum(decays, axis=-1)
    mine = lax.dynamic_index_in_dim(decays, x, 1, keepdims=False)
    mine = lax.dynamic_index_in_dim(mine, c, 1, keepdims=False)

    grouped = gather(line, inputs, qkv_weight, head_size)
    grouped = grouped.reshape(3, line * heads, chunk, head_size)
    cumulated = running(mine.reshape(line * heads, chunk))
    intra_term, update, _, queries_decayed = block_terms(
        grouped[0], grouped[1], grouped[2], cumulated
    )
    update = update.reshape(line, heads, head_size, head_size)
    flat = [(d, s) for d in range(dps) for s in range(seqs)]
    core_pairs = [(d * seqs + s, d * seqs + (s ^ 1)) for d, s in flat]
    x_pairs = [(d * seqs + s, (d ^ 1) * seqs + s) for d, s in flat]
    other = lax.ppermute(update, ("dp", "seq"), core_pairs)
    lower = jnp.where(c == 0, update, other)
    upper = jnp.where(c == 0, other, update)
    my_totals = lax.dynamic_index_in_dim(totals, x, 1, keepdims=False)
    joined = jnp.exp(my_totals[:, 1])[..., None, None] * lower + upper
    part = lax.dynamic_slice_in_dim(joined, 2 * c, 2, axis=1)
    part = lax.ppermute(part, ("dp", "seq"), x_pairs)
    part_other = lax.ppermute(part, ("dp", "seq"), core_pairs)
    across = jnp.concatenate(
        [jnp.where(c == 0, part, part_other), jnp.where(c == 0, part_other, part)], axis=1
    )
    state = jnp.zeros_like(update[0])
    block_totals = totals[:, :, 0] + totals[:, :, 1]
    carried = []
    for zz in range(line):
        starts = []
        for xx in (0, 1):
            starts.append(state)
            term = jnp.where(x == xx, joined[zz], across[zz])
            state = jnp.exp(block_totals[zz, xx])[:, None, None] * state + term
        start = jnp.where(x == 0, starts[0], starts[1])
        later = jnp.exp(my_totals[zz, 0])[:, None, None] * start + lower[zz]
        carried.append(jnp.where(c == 0, start, later))
    carried = jnp.concatenate(carried, axis=0)
    normed = finish_heads(intra_term, queries_decayed, carried, jnp.tile(gains, (line, 1)))
    tiles = normed.astype(jnp.bfloat16).reshape(line, 2, 2, chunk, head_size)
    tiles = jnp.transpose(tiles, (0, 1, 3, 2, 4)).reshape(line, 2, chunk, 2 * head_size)
    return scatter(line, tiles)


def solution(mesh):
    in_specs = (P("seq", None), P(None, ("dp", "seq")), P("dp", "seq"), P("dp", None))
    out_specs = P("seq", "dp")

    def shards(inputs, qkv_weight, log_decay, out_gain):
        local_heads, head_size = out_gain.shape
        whole_heads = qkv_weight.shape[1] == 3 * head_size
        fits = whole_heads and local_heads == mesh.shape["seq"] and mesh.shape["dp"] == 4
        body = shards_quarter if fits else shards_wide
        return body(inputs, qkv_weight, log_decay, out_gain)

    return jax.shard_map(shards, mesh=mesh, in_specs=in_specs, out_specs=out_specs, check_vma=False)
```

```python
import functools

import jax
import jax.numpy as jnp
from jax import lax
from jax.experimental import pallas as pl
from jax.experimental.pallas import tpu as pltpu
from jax.sharding import PartitionSpec as P

MESH = pl.DeviceIdType.MESH
SUBS = 4


def prefix_2(value, axis, join, neutral):
    count, mine = (lax.axis_size(axis), lax.axis_index(axis))
    pieces = jax.tree.map(lambda part: lax.all_gather(part, axis), value)
    subtotal = jax.tree.map(
        lambda part, zero: jnp.full_like(part, 0) + jnp.asarray(zero, part.dtype), value, neutral
    )

    def turn(position, subtotal):
        longer = join(subtotal, jax.tree.map(lambda part: part[position], pieces))
        return jax.tree.map(lambda new, old: jnp.where(position < mine, new, old), longer, subtotal)

    return lax.fori_loop(0, count - 1, turn, subtotal)


def running(decays):
    index = jnp.arange(decays.shape[-1])
    upto = (index[:, None] <= index[None, :]).astype(jnp.float32)
    return jnp.dot(decays, upto, precision=lax.Precision.HIGHEST)


def block_terms(queries, keys, values, cumulated):
    tok_count = queries.shape[-2]
    row_index = jnp.arange(tok_count)[:, None]
    col_index = jnp.arange(tok_count)[None, :]
    causal = row_index >= col_index
    spread = cumulated[:, :, None] - cumulated[:, None, :]
    decay_mask = jnp.where(causal, jnp.exp(jnp.where(causal, spread, 0.0)), 0.0)
    scores = jnp.einsum("htd,hsd->hts", queries, keys, preferred_element_type=jnp.float32)
    weights = (scores * decay_mask).astype(jnp.bfloat16)
    intra_term = jnp.einsum("hts,hsd->htd", weights, values, preferred_element_type=jnp.float32)
    tail_decay = jnp.exp(cumulated[:, -1:] - cumulated)
    keys_decayed = keys.astype(jnp.float32) * tail_decay[:, :, None]
    update = jnp.einsum(
        "hsd,hse->hde", keys_decayed, values.astype(jnp.float32), precision=lax.Precision.HIGHEST
    )
    block_total = cumulated[:, -1]
    queries_decayed = queries.astype(jnp.float32) * jnp.exp(cumulated)[:, :, None]
    return (intra_term, update, block_total, queries_decayed)


def finish_heads(intra_term, queries_decayed, carried, gains):
    outer_term = jnp.einsum(
        "htd,hde->hte", queries_decayed, carried, precision=lax.Precision.HIGHEST
    )
    combined = intra_term + outer_term
    root_mean = lax.rsqrt(jnp.mean(combined * combined, axis=-1, keepdims=True) + 1e-05)
    return combined * root_mean * gains[:, None, :]


def chain_combine(earlier_pair, later_pair):
    return (
        earlier_pair[0] + later_pair[0],
        jnp.exp(later_pair[0])[:, None, None] * earlier_pair[1] + later_pair[1],
    )


def shards_wide(inputs, qkv_weight, log_decay, out_gain):
    tok_count = inputs.shape[0]
    local_heads = out_gain.shape[0]
    head_size = out_gain.shape[1]
    projected = jnp.dot(
        inputs,
        lax.all_gather(qkv_weight, "seq", axis=1, tiled=True),
        preferred_element_type=jnp.float32,
    )
    activated = jax.nn.silu(projected).astype(jnp.bfloat16)
    grouped = jnp.transpose(activated.reshape(tok_count, local_heads, 3, head_size), (2, 1, 0, 3))
    intra_term, update, block_total, queries_decayed = block_terms(
        grouped[0], grouped[1], grouped[2], running(log_decay)
    )
    identity = (jnp.zeros_like(block_total), jnp.zeros_like(update))
    prefix = prefix_2((block_total, update), "seq", chain_combine, identity)
    normed = finish_heads(intra_term, queries_decayed, prefix[1], out_gain)
    return (
        jnp.transpose(normed, (1, 0, 2))
        .reshape(tok_count, local_heads * head_size)
        .astype(jnp.bfloat16)
    )


def place():
    dp, seq = lax.axis_index("dp"), lax.axis_index("seq")
    return dp, seq, dp // 2, dp % 2, seq // 2, seq % 2


def gather_kernel(
    line, x_ref, w_ref, l_ref, g_ref, out, ld, gd, xg, wg, total,
    l_send, l_recv, g_send, g_recv, l_local_sem, own_send, own_recv, first_send, z_send, z_recv, y_send, y_recv,
    wx_send, wx_recv, wf_send, wf_recv, wp_send, wp_recv, local_sem,
):
    dp, seq, y, x, z, c = place()
    rows = x_ref.shape[0] // 2
    half = rows // 2
    sub = half // SUBS
    width = w_ref.shape[1]
    pieces = (line - 1) * SUBS
    depth = w_ref.shape[0] // pieces
    x_pair = {"dp": dp + 1 - 2 * x, "seq": seq}
    y_pair = {"dp": dp + 2 - 4 * y, "seq": seq}
    c_pair = {"dp": dp, "seq": seq + 1 - 2 * c}

    def at(position, core):
        return {"dp": dp, "seq": 2 * position + core}

    seqs = ld.shape[1]

    def device(xx, ss):
        return {"dp": 2 * y + xx, "seq": ss}

    def others(act):
        for xx in (0, 1):
            for ss in range(seqs):
                @pl.when((xx != x) | (ss != seq))
                def _():
                    act(xx, ss)

    barrier = pltpu.get_barrier_semaphore()
    others(
        lambda xx, ss: pl.semaphore_signal(
            barrier, inc=1, device_id=device(xx, ss), device_id_type=MESH
        )
    )
    pl.semaphore_signal(barrier, inc=1, device_id=y_pair, device_id_type=MESH)
    pl.semaphore_wait(barrier, 2 * seqs)

    def push(xx, ss):
        return pltpu.make_async_remote_copy(
            src_ref=l_ref, dst_ref=ld.at[x, seq],
            send_sem=l_send.at[xx, ss], recv_sem=l_recv.at[x, seq],
            device_id=device(xx, ss), device_id_type=MESH,
        )

    def pull(xx, ss):
        return pltpu.make_async_remote_copy(
            src_ref=l_ref, dst_ref=ld.at[xx, ss],
            send_sem=l_send.at[xx, ss], recv_sem=l_recv.at[xx, ss],
            device_id=device(xx, ss), device_id_type=MESH,
        )

    gain = pltpu.make_async_remote_copy(
        src_ref=g_ref, dst_ref=gd.at[x], send_sem=g_send, recv_sem=g_recv,
        device_id=device(1 - x, seq), device_id_type=MESH,
    )
    l_local = pltpu.make_async_copy(l_ref, ld.at[x, seq], l_local_sem.at[0])
    g_local = pltpu.make_async_copy(g_ref, gd.at[x], l_local_sem.at[1])
    def remote(src, dst, send, recv, target):
        return pltpu.make_async_remote_copy(
            src_ref=src, dst_ref=dst, send_sem=send, recv_sem=recv,
            device_id=target, device_id_type=MESH,
        )

    def strip(position, side, r):
        return xg.at[position, pl.ds(pl.multiple_of(side * half + r * sub, sub), sub)]

    def first(core, step, r):
        start = pl.multiple_of(core * rows + y * half + r * sub, sub)
        return remote(
            x_ref.at[pl.ds(start, sub)], strip(z, y, r),
            first_send.at[core, (step + 1) // 2, r], z_recv.at[z, r], at(z + step, core),
        )

    def columns(xx, cc):
        return pl.ds(pl.multiple_of((xx * 2 + cc) * width, 128), width)

    def weight_first(j):
        part = pl.ds(j * depth, depth)
        return remote(
            w_ref.at[part], wg.at[part, columns(x, c)], wx_send.at[j], wx_recv.at[j], x_pair
        )

    def weight_next(j):
        part = wg.at[pl.ds(j * depth, depth), columns(1 - x, c)]
        return remote(part, part, wf_send.at[j], wf_recv.at[j], c_pair)

    def own_rows(core):
        return x_ref.at[pl.ds(pl.multiple_of(core * rows, rows), rows)]

    own_local = pltpu.make_async_copy(own_rows(c), xg.at[z], local_sem.at[0])
    own_peer = remote(own_rows(1 - c), xg.at[z], own_send, own_recv, c_pair)
    w_local = pltpu.make_async_copy(w_ref, wg.at[:, columns(x, c)], local_sem.at[1])
    w_peer = remote(w_ref, wg.at[:, columns(x, c)], wp_send, wp_recv, c_pair)

    def exists(position):
        return (position >= 0) & (position < line)

    for r in range(SUBS):
        for step in (1, -1):
            @pl.when((c == x) & exists(z + step))
            def _():
                for core in (0, 1):
                    first(core, step, r).start()
    for j in range(pieces):
        weight_first(j).start()

    @pl.when(c == x)
    def _():
        own_local.start()
        own_peer.start()
    w_peer.start()
    w_local.start()
    others(lambda xx, ss: push(xx, ss).start())
    gain.start()
    l_local.start()
    g_local.start()

    def z_next(origin, step, r):
        part = strip(origin, y, r)
        return remote(part, part, z_send.at[origin, r], z_recv.at[origin, r], at(z - step, c))

    def y_next(origin, side, r):
        part = strip(origin, side, r)
        return remote(part, part, y_send.at[origin, r], y_recv.at[origin, r], y_pair)

    model = w_ref.shape[0]
    early = (line - 2) * SUBS * depth
    tile = 2 * out.shape[4]

    def project(position, xx, low, high, begin=False, resume=False):
        def turn(n, carry):
            start = pl.multiple_of(n * tile, 128)
            cols = pl.ds(pl.multiple_of(xx * 2 * width + n * tile, 128), tile)
            term = jnp.dot(
                xg[position, :, low:high], wg[low:high, cols], preferred_element_type=jnp.float32
            )
            if begin:
                total[position, :, pl.ds(start, tile)] = term
                return carry
            if resume:
                term = term + total[position, :, pl.ds(start, tile)]
            term = (term * jax.nn.sigmoid(term)).astype(out.dtype)
            for i in (0, 1):
                j = 2 * n + i
                out[j % 3, position, 2 * xx + j // 3] = term[:, i * tile // 2 : (i + 1) * tile // 2]
            return carry

        lax.fori_loop(0, 2 * width // tile, turn, 0)

    def around(k, act):
        for step in (1, -1):
            @pl.when(exists(z + step * k))
            def _():
                act(z + step * k)

    def y_wait(k):
        def act(origin):
            for r in range(SUBS):
                y_next(origin, 1 - y, r).wait_recv()

        around(k, act)

    @pl.when(c == x)
    def _():
        own_local.wait()

    @pl.when(c != x)
    def _():
        own_peer.wait_recv()

    w_local.wait()
    w_peer.wait()
    project(z, x, 0, model)

    for k in range(1, line):
        for r in range(SUBS):
            for step in (1, -1):
                origin = z + step * k

                @pl.when(exists(origin))
                def _():
                    z_next(origin, step, r).wait_recv()
                    y_next(origin, y, r).start()

                    @pl.when(exists(z - step))
                    def _():
                        z_next(origin, step, r).start()
            j = (k - 1) * SUBS + r
            weight_first(j).wait_recv()
            weight_next(j).start()
            if k >= 2 and r == 1:
                y_wait(k - 1)
                around(k - 1, lambda origin: project(origin, x, 0, model))
                if k == line - 1:
                    around(k - 1, lambda origin: project(origin, 1 - x, 0, early, begin=True))
        if k == line - 2:
            for j in range((line - 2) * SUBS):
                weight_next(j).wait_recv()
            project(z, 1 - x, 0, early, begin=True)
            for before in range(1, k):
                around(before, lambda origin: project(origin, 1 - x, 0, early, begin=True))

    for j in range((line - 2) * SUBS, pieces):
        weight_next(j).wait_recv()
    project(z, 1 - x, early, model, resume=True)
    for k in range(1, line - 1):
        around(k, lambda origin: project(origin, 1 - x, early, model, resume=True))
    y_wait(line - 1)
    around(line - 1, lambda origin: project(origin, x, 0, model))
    around(line - 1, lambda origin: project(origin, 1 - x, 0, model))

    for k in range(1, line):
        for r in range(SUBS):
            for step in (1, -1):
                origin = z + step * k

                @pl.when(exists(origin))
                def _():
                    y_next(origin, y, r).wait_send()

                    @pl.when(exists(z - step))
                    def _():
                        z_next(origin, step, r).wait_send()
            j = (k - 1) * SUBS + r
            weight_first(j).wait_send()
            weight_next(j).wait_send()
    for r in range(SUBS):
        for step in (1, -1):
            @pl.when((c == x) & exists(z + step))
            def _():
                for core in (0, 1):
                    first(core, step, r).wait_send()

    @pl.when(c == x)
    def _():
        own_peer.wait_send()
    others(lambda xx, ss: pull(xx, ss).wait_recv())
    others(lambda xx, ss: push(xx, ss).wait_send())
    gain.wait()
    l_local.wait()
    g_local.wait()


def gather(line, inputs, weight, log_decay, out_gain):
    tok, depth = inputs.shape
    dma = pltpu.SemaphoreType.DMA
    pieces = (line - 1) * SUBS
    width = weight.shape[1]
    head_size = out_gain.shape[1]
    any_space = pl.BlockSpec(memory_space=pl.ANY)
    vmem = pl.BlockSpec(memory_space=pltpu.VMEM)
    return pl.pallas_call(
        functools.partial(gather_kernel, line),
        out_shape=(
            jax.ShapeDtypeStruct((3, line, 4, tok // 2, head_size), inputs.dtype),
            jax.ShapeDtypeStruct((2, 2 * line) + log_decay.shape, log_decay.dtype),
            jax.ShapeDtypeStruct((2,) + out_gain.shape, out_gain.dtype),
        ),
        in_specs=[any_space, any_space, vmem, vmem],
        out_specs=(vmem, vmem, vmem),
        scratch_shapes=[
            pltpu.VMEM((line, tok // 2, depth), inputs.dtype),
            pltpu.VMEM((depth, 4 * width), weight.dtype),
            pltpu.VMEM((line, tok // 2, 2 * width), jnp.float32),
            dma((2, 2 * line)), dma((2, 2 * line)), dma, dma, dma((2,)),
            dma, dma, dma((2, 2, SUBS)), dma((line, SUBS)), dma((line, SUBS)),
            dma((line, SUBS)), dma((line, SUBS)),
            dma((pieces,)), dma((pieces,)), dma((pieces,)), dma((pieces,)),
            dma, dma, dma((2,)),
        ],
        compiler_params=pltpu.CompilerParams(
            collective_id=0, has_side_effects=True, vmem_limit_bytes=50 << 20
        ),
        name="gather",
    )(inputs, weight, log_decay, out_gain)


def scatter_kernel(line, tiles, out, send_sem, recv_sem, local_sem):
    dp, seq, y, x, z, c = place()
    rows, cols = tiles.shape[2], tiles.shape[3]

    def device(xx, zz, cc):
        return {"dp": 2 * y + xx, "seq": 2 * zz + cc}

    barrier = pltpu.get_barrier_semaphore()
    for zz in range(line):
        for cc in (0, 1):
            @pl.when((zz != z) | (cc != c) | (c != x))
            def _():
                pl.semaphore_signal(
                    barrier, inc=1, device_id=device(c, zz, cc), device_id_type=MESH
                )
    pl.semaphore_wait(barrier, 2 * line - (c == x).astype(jnp.int32))

    def area(zz, cc):
        return out.at[
            pl.ds(pl.multiple_of(cc * rows, rows), rows),
            pl.ds(pl.multiple_of(zz * cols, 128), cols),
        ]

    def push(zz, xx):
        return pltpu.make_async_remote_copy(
            src_ref=tiles.at[zz, xx], dst_ref=area(z, c),
            send_sem=send_sem.at[zz, xx], recv_sem=recv_sem.at[z, c],
            device_id=device(xx, zz, x), device_id_type=MESH,
        )

    def pull(zz, cc):
        return pltpu.make_async_remote_copy(
            src_ref=tiles.at[0, 0], dst_ref=area(zz, cc),
            send_sem=send_sem.at[0, 0], recv_sem=recv_sem.at[zz, cc],
            device_id=device(1 - x, z, c), device_id_type=MESH,
        )

    local = pltpu.make_async_copy(tiles.at[z, x], area(z, c), local_sem)
    own = c == x
    for zz in range(line):
        for xx in (0, 1):
            @pl.when((zz != z) | (xx != x) | jnp.logical_not(own))
            def _():
                push(zz, xx).start()

    @pl.when(own)
    def _():
        local.start()
    for zz in range(line):
        for cc in (0, 1):
            @pl.when((zz != z) | (cc != c) | jnp.logical_not(own))
            def _():
                pull(zz, cc).wait_recv()
    for zz in range(line):
        for xx in (0, 1):
            @pl.when((zz != z) | (xx != x) | jnp.logical_not(own))
            def _():
                push(zz, xx).wait_send()

    @pl.when(own)
    def _():
        local.wait()


def scatter(line, tiles):
    dma = pltpu.SemaphoreType.DMA
    _, _, rows, cols = tiles.shape
    any_space = pl.BlockSpec(memory_space=pl.ANY)
    return pl.pallas_call(
        functools.partial(scatter_kernel, line),
        out_shape=jax.ShapeDtypeStruct((2 * rows, line * cols), tiles.dtype),
        in_specs=[any_space],
        out_specs=any_space,
        scratch_shapes=[dma((line, 2)), dma((line, 2)), dma],
        compiler_params=pltpu.CompilerParams(
            collective_id=1, has_side_effects=True, vmem_limit_bytes=1 << 20
        ),
        name="scatter",
    )(tiles)


def shards_quarter(inputs, qkv_weight, log_decay, out_gain):
    dps, seqs = lax.axis_size("dp"), lax.axis_size("seq")
    dp, seq, y, x, z, c = place()
    line = seqs // 2
    tok = inputs.shape[0]
    chunk = tok // 2
    local_heads, head_size = out_gain.shape
    heads = 4
    grouped, decays, gains = gather(line, inputs, qkv_weight, log_decay, out_gain)
    decays = lax.dynamic_slice_in_dim(decays, 2 * z, 2, axis=2)
    decays = jnp.transpose(decays, (1, 0, 2, 3)).reshape(line, 2, 2, 2, 2, chunk)
    decays = jnp.transpose(decays, (0, 1, 4, 2, 3, 5)).reshape(line, 2, 2, heads, chunk)
    gains = lax.dynamic_slice_in_dim(gains, 2 * z, 2, axis=1).reshape(heads, head_size)
    totals = jnp.sum(decays, axis=-1)
    mine = lax.dynamic_index_in_dim(decays, x, 1, keepdims=False)
    mine = lax.dynamic_index_in_dim(mine, c, 1, keepdims=False)

    grouped = grouped.reshape(3, line * heads, chunk, head_size)
    cumulated = running(mine.reshape(line * heads, chunk))
    intra_term, update, _, queries_decayed = block_terms(
        grouped[0], grouped[1], grouped[2], cumulated
    )
    update = update.reshape(line, heads, head_size, head_size)
    flat = [(d, s) for d in range(dps) for s in range(seqs)]
    core_pairs = [(d * seqs + s, d * seqs + (s ^ 1)) for d, s in flat]
    x_pairs = [(d * seqs + s, (d ^ 1) * seqs + s) for d, s in flat]
    other = lax.ppermute(update, ("dp", "seq"), core_pairs)
    lower = jnp.where(c == 0, update, other)
    upper = jnp.where(c == 0, other, update)
    my_totals = lax.dynamic_index_in_dim(totals, x, 1, keepdims=False)
    joined = jnp.exp(my_totals[:, 1])[..., None, None] * lower + upper
    part = lax.dynamic_slice_in_dim(joined, 2 * c, 2, axis=1)
    part = lax.ppermute(part, ("dp", "seq"), x_pairs)
    part_other = lax.ppermute(part, ("dp", "seq"), core_pairs)
    across = jnp.concatenate(
        [jnp.where(c == 0, part, part_other), jnp.where(c == 0, part_other, part)], axis=1
    )
    state = jnp.zeros_like(update[0])
    block_totals = totals[:, :, 0] + totals[:, :, 1]
    carried = []
    for zz in range(line):
        starts = []
        for xx in (0, 1):
            starts.append(state)
            term = jnp.where(x == xx, joined[zz], across[zz])
            state = jnp.exp(block_totals[zz, xx])[:, None, None] * state + term
        start = jnp.where(x == 0, starts[0], starts[1])
        later = jnp.exp(my_totals[zz, 0])[:, None, None] * start + lower[zz]
        carried.append(jnp.where(c == 0, start, later))
    carried = jnp.concatenate(carried, axis=0)
    normed = finish_heads(intra_term, queries_decayed, carried, jnp.tile(gains, (line, 1)))
    tiles = normed.astype(jnp.bfloat16).reshape(line, 2, 2, chunk, head_size)
    tiles = jnp.transpose(tiles, (0, 1, 3, 2, 4)).reshape(line, 2, chunk, 2 * head_size)
    return scatter(line, tiles)


def solution(mesh):
    in_specs = (P("seq", None), P(None, ("dp", "seq")), P("dp", "seq"), P("dp", None))
    out_specs = P("seq", "dp")

    def shards(inputs, qkv_weight, log_decay, out_gain):
        local_heads, head_size = out_gain.shape
        whole_heads = qkv_weight.shape[1] == 3 * head_size
        fits = whole_heads and local_heads == mesh.shape["seq"] and mesh.shape["dp"] == 4
        body = shards_quarter if fits else shards_wide
        return body(inputs, qkv_weight, log_decay, out_gain)

    return jax.shard_map(shards, mesh=mesh, in_specs=in_specs, out_specs=out_specs, check_vma=False)
```

```python
import functools

import jax
import jax.numpy as jnp
from jax import lax
from jax.experimental import pallas as pl
from jax.experimental.pallas import tpu as pltpu
from jax.sharding import PartitionSpec as P

MESH = pl.DeviceIdType.MESH
SUBS = 8


def prefix_2(value, axis, join, neutral):
    count, mine = (lax.axis_size(axis), lax.axis_index(axis))
    pieces = jax.tree.map(lambda part: lax.all_gather(part, axis), value)
    subtotal = jax.tree.map(
        lambda part, zero: jnp.full_like(part, 0) + jnp.asarray(zero, part.dtype), value, neutral
    )

    def turn(position, subtotal):
        longer = join(subtotal, jax.tree.map(lambda part: part[position], pieces))
        return jax.tree.map(lambda new, old: jnp.where(position < mine, new, old), longer, subtotal)

    return lax.fori_loop(0, count - 1, turn, subtotal)


def running(decays):
    index = jnp.arange(decays.shape[-1])
    upto = (index[:, None] <= index[None, :]).astype(jnp.float32)
    return jnp.dot(decays, upto, precision=lax.Precision.HIGHEST)


def block_terms(queries, keys, values, cumulated):
    tok_count = queries.shape[-2]
    row_index = jnp.arange(tok_count)[:, None]
    col_index = jnp.arange(tok_count)[None, :]
    causal = row_index >= col_index
    spread = cumulated[:, :, None] - cumulated[:, None, :]
    decay_mask = jnp.where(causal, jnp.exp(jnp.where(causal, spread, 0.0)), 0.0)
    scores = jnp.einsum("htd,hsd->hts", queries, keys, preferred_element_type=jnp.float32)
    weights = (scores * decay_mask).astype(jnp.bfloat16)
    intra_term = jnp.einsum("hts,hsd->htd", weights, values, preferred_element_type=jnp.float32)
    tail_decay = jnp.exp(cumulated[:, -1:] - cumulated)
    keys_decayed = keys.astype(jnp.float32) * tail_decay[:, :, None]
    update = jnp.einsum(
        "hsd,hse->hde", keys_decayed, values.astype(jnp.float32), precision=lax.Precision.HIGHEST
    )
    block_total = cumulated[:, -1]
    queries_decayed = queries.astype(jnp.float32) * jnp.exp(cumulated)[:, :, None]
    return (intra_term, update, block_total, queries_decayed)


def finish_heads(intra_term, queries_decayed, carried, gains):
    outer_term = jnp.einsum(
        "htd,hde->hte", queries_decayed, carried, precision=lax.Precision.HIGHEST
    )
    combined = intra_term + outer_term
    root_mean = lax.rsqrt(jnp.mean(combined * combined, axis=-1, keepdims=True) + 1e-05)
    return combined * root_mean * gains[:, None, :]


def chain_combine(earlier_pair, later_pair):
    return (
        earlier_pair[0] + later_pair[0],
        jnp.exp(later_pair[0])[:, None, None] * earlier_pair[1] + later_pair[1],
    )


def shards_wide(inputs, qkv_weight, log_decay, out_gain):
    tok_count = inputs.shape[0]
    local_heads = out_gain.shape[0]
    head_size = out_gain.shape[1]
    projected = jnp.dot(
        inputs,
        lax.all_gather(qkv_weight, "seq", axis=1, tiled=True),
        preferred_element_type=jnp.float32,
    )
    activated = jax.nn.silu(projected).astype(jnp.bfloat16)
    grouped = jnp.transpose(activated.reshape(tok_count, local_heads, 3, head_size), (2, 1, 0, 3))
    intra_term, update, block_total, queries_decayed = block_terms(
        grouped[0], grouped[1], grouped[2], running(log_decay)
    )
    identity = (jnp.zeros_like(block_total), jnp.zeros_like(update))
    prefix = prefix_2((block_total, update), "seq", chain_combine, identity)
    normed = finish_heads(intra_term, queries_decayed, prefix[1], out_gain)
    return (
        jnp.transpose(normed, (1, 0, 2))
        .reshape(tok_count, local_heads * head_size)
        .astype(jnp.bfloat16)
    )


def place():
    dp, seq = lax.axis_index("dp"), lax.axis_index("seq")
    return dp, seq, dp // 2, dp % 2, seq // 2, seq % 2


def gather_kernel(
    line, x_ref, w_ref, l_ref, g_ref, out, ld, gd, xg, wg, total,
    l_send, l_recv, g_send, g_recv, l_local_sem, own_send, own_recv, first_send, z_send, z_recv, y_send, y_recv,
    wx_send, wx_recv, wf_send, wf_recv, wp_send, wp_recv, local_sem,
):
    dp, seq, y, x, z, c = place()
    rows = x_ref.shape[0] // 2
    half = rows // 2
    sub = half // SUBS
    width = w_ref.shape[1]
    pieces = (line - 1) * SUBS
    depth = w_ref.shape[0] // pieces
    x_pair = {"dp": dp + 1 - 2 * x, "seq": seq}
    y_pair = {"dp": dp + 2 - 4 * y, "seq": seq}
    c_pair = {"dp": dp, "seq": seq + 1 - 2 * c}

    def at(position, core):
        return {"dp": dp, "seq": 2 * position + core}

    seqs = ld.shape[1]

    def device(xx, ss):
        return {"dp": 2 * y + xx, "seq": ss}

    def others(act):
        for xx in (0, 1):
            for ss in range(seqs):
                @pl.when((xx != x) | (ss != seq))
                def _():
                    act(xx, ss)

    barrier = pltpu.get_barrier_semaphore()
    others(
        lambda xx, ss: pl.semaphore_signal(
            barrier, inc=1, device_id=device(xx, ss), device_id_type=MESH
        )
    )
    pl.semaphore_signal(barrier, inc=1, device_id=y_pair, device_id_type=MESH)
    pl.semaphore_wait(barrier, 2 * seqs)

    def push(xx, ss):
        return pltpu.make_async_remote_copy(
            src_ref=l_ref, dst_ref=ld.at[x, seq],
            send_sem=l_send.at[xx, ss], recv_sem=l_recv.at[x, seq],
            device_id=device(xx, ss), device_id_type=MESH,
        )

    def pull(xx, ss):
        return pltpu.make_async_remote_copy(
            src_ref=l_ref, dst_ref=ld.at[xx, ss],
            send_sem=l_send.at[xx, ss], recv_sem=l_recv.at[xx, ss],
            device_id=device(xx, ss), device_id_type=MESH,
        )

    gain = pltpu.make_async_remote_copy(
        src_ref=g_ref, dst_ref=gd.at[x], send_sem=g_send, recv_sem=g_recv,
        device_id=device(1 - x, seq), device_id_type=MESH,
    )
    l_local = pltpu.make_async_copy(l_ref, ld.at[x, seq], l_local_sem.at[0])
    g_local = pltpu.make_async_copy(g_ref, gd.at[x], l_local_sem.at[1])
    def remote(src, dst, send, recv, target):
        return pltpu.make_async_remote_copy(
            src_ref=src, dst_ref=dst, send_sem=send, recv_sem=recv,
            device_id=target, device_id_type=MESH,
        )

    def strip(position, side, r):
        return xg.at[position, pl.ds(pl.multiple_of(side * half + r * sub, sub), sub)]

    def first(core, step, r):
        start = pl.multiple_of(core * rows + y * half + r * sub, sub)
        return remote(
            x_ref.at[pl.ds(start, sub)], strip(z, y, r),
            first_send.at[core, (step + 1) // 2, r], z_recv.at[z, r], at(z + step, core),
        )

    def columns(xx, cc):
        return pl.ds(pl.multiple_of((xx * 2 + cc) * width, 128), width)

    def weight_first(j):
        part = pl.ds(j * depth, depth)
        return remote(
            w_ref.at[part], wg.at[part, columns(x, c)], wx_send.at[j], wx_recv.at[j], x_pair
        )

    def weight_next(j):
        part = wg.at[pl.ds(j * depth, depth), columns(1 - x, c)]
        return remote(part, part, wf_send.at[j], wf_recv.at[j], c_pair)

    def own_rows(core):
        return x_ref.at[pl.ds(pl.multiple_of(core * rows, rows), rows)]

    own_local = pltpu.make_async_copy(own_rows(c), xg.at[z], local_sem.at[0])
    own_peer = remote(own_rows(1 - c), xg.at[z], own_send, own_recv, c_pair)
    w_local = pltpu.make_async_copy(w_ref, wg.at[:, columns(x, c)], local_sem.at[1])
    w_peer = remote(w_ref, wg.at[:, columns(x, c)], wp_send, wp_recv, c_pair)

    def exists(position):
        return (position >= 0) & (position < line)

    for r in range(SUBS):
        for step in (1, -1):
            @pl.when((c == x) & exists(z + step))
            def _():
                for core in (0, 1):
                    first(core, step, r).start()
    for j in range(pieces):
        weight_first(j).start()

    @pl.when(c == x)
    def _():
        own_local.start()
        own_peer.start()
    w_peer.start()
    w_local.start()
    others(lambda xx, ss: push(xx, ss).start())
    gain.start()
    l_local.start()
    g_local.start()

    def z_next(origin, step, r):
        part = strip(origin, y, r)
        return remote(part, part, z_send.at[origin, r], z_recv.at[origin, r], at(z - step, c))

    def y_next(origin, side, r):
        part = strip(origin, side, r)
        return remote(part, part, y_send.at[origin, r], y_recv.at[origin, r], y_pair)

    model = w_ref.shape[0]
    early = (line - 2) * SUBS * depth
    tile = 2 * out.shape[4]

    def project(position, xx, low, high, begin=False, resume=False):
        def turn(n, carry):
            start = pl.multiple_of(n * tile, 128)
            cols = pl.ds(pl.multiple_of(xx * 2 * width + n * tile, 128), tile)
            term = jnp.dot(
                xg[position, :, low:high], wg[low:high, cols], preferred_element_type=jnp.float32
            )
            if begin:
                total[position, :, pl.ds(start, tile)] = term
                return carry
            if resume:
                term = term + total[position, :, pl.ds(start, tile)]
            term = (term * jax.nn.sigmoid(term)).astype(out.dtype)
            for i in (0, 1):
                j = 2 * n + i
                out[j % 3, position, 2 * xx + j // 3] = term[:, i * tile // 2 : (i + 1) * tile // 2]
            return carry

        lax.fori_loop(0, 2 * width // tile, turn, 0)

    def around(k, act):
        for step in (1, -1):
            @pl.when(exists(z + step * k))
            def _():
                act(z + step * k)

    def y_wait(k):
        def act(origin):
            for r in range(SUBS):
                y_next(origin, 1 - y, r).wait_recv()

        around(k, act)

    @pl.when(c == x)
    def _():
        own_local.wait()

    @pl.when(c != x)
    def _():
        own_peer.wait_recv()

    w_local.wait()
    w_peer.wait()
    project(z, x, 0, model)

    for k in range(1, line):
        for r in range(SUBS):
            for step in (1, -1):
                origin = z + step * k

                @pl.when(exists(origin))
                def _():
                    z_next(origin, step, r).wait_recv()
                    y_next(origin, y, r).start()

                    @pl.when(exists(z - step))
                    def _():
                        z_next(origin, step, r).start()
            j = (k - 1) * SUBS + r
            weight_first(j).wait_recv()
            weight_next(j).start()
            if k >= 2 and r == SUBS // 2 - 1:
                y_wait(k - 1)
                around(k - 1, lambda origin: project(origin, x, 0, model))
                if k == line - 1:
                    around(k - 1, lambda origin: project(origin, 1 - x, 0, early, begin=True))
        if k == line - 2:
            for j in range((line - 2) * SUBS):
                weight_next(j).wait_recv()
            project(z, 1 - x, 0, early, begin=True)
            for before in range(1, k):
                around(before, lambda origin: project(origin, 1 - x, 0, early, begin=True))

    for j in range((line - 2) * SUBS, pieces):
        weight_next(j).wait_recv()
    project(z, 1 - x, early, model, resume=True)
    for k in range(1, line - 1):
        around(k, lambda origin: project(origin, 1 - x, early, model, resume=True))
    y_wait(line - 1)
    around(line - 1, lambda origin: project(origin, x, 0, model))
    around(line - 1, lambda origin: project(origin, 1 - x, 0, model))

    for k in range(1, line):
        for r in range(SUBS):
            for step in (1, -1):
                origin = z + step * k

                @pl.when(exists(origin))
                def _():
                    y_next(origin, y, r).wait_send()

                    @pl.when(exists(z - step))
                    def _():
                        z_next(origin, step, r).wait_send()
            j = (k - 1) * SUBS + r
            weight_first(j).wait_send()
            weight_next(j).wait_send()
    for r in range(SUBS):
        for step in (1, -1):
            @pl.when((c == x) & exists(z + step))
            def _():
                for core in (0, 1):
                    first(core, step, r).wait_send()

    @pl.when(c == x)
    def _():
        own_peer.wait_send()
    others(lambda xx, ss: pull(xx, ss).wait_recv())
    others(lambda xx, ss: push(xx, ss).wait_send())
    gain.wait()
    l_local.wait()
    g_local.wait()


def gather(line, inputs, weight, log_decay, out_gain):
    tok, depth = inputs.shape
    dma = pltpu.SemaphoreType.DMA
    pieces = (line - 1) * SUBS
    width = weight.shape[1]
    head_size = out_gain.shape[1]
    any_space = pl.BlockSpec(memory_space=pl.ANY)
    vmem = pl.BlockSpec(memory_space=pltpu.VMEM)
    return pl.pallas_call(
        functools.partial(gather_kernel, line),
        out_shape=(
            jax.ShapeDtypeStruct((3, line, 4, tok // 2, head_size), inputs.dtype),
            jax.ShapeDtypeStruct((2, 2 * line) + log_decay.shape, log_decay.dtype),
            jax.ShapeDtypeStruct((2,) + out_gain.shape, out_gain.dtype),
        ),
        in_specs=[any_space, any_space, vmem, vmem],
        out_specs=(vmem, vmem, vmem),
        scratch_shapes=[
            pltpu.VMEM((line, tok // 2, depth), inputs.dtype),
            pltpu.VMEM((depth, 4 * width), weight.dtype),
            pltpu.VMEM((line, tok // 2, 2 * width), jnp.float32),
            dma((2, 2 * line)), dma((2, 2 * line)), dma, dma, dma((2,)),
            dma, dma, dma((2, 2, SUBS)), dma((line, SUBS)), dma((line, SUBS)),
            dma((line, SUBS)), dma((line, SUBS)),
            dma((pieces,)), dma((pieces,)), dma((pieces,)), dma((pieces,)),
            dma, dma, dma((2,)),
        ],
        compiler_params=pltpu.CompilerParams(
            collective_id=0, has_side_effects=True, vmem_limit_bytes=50 << 20
        ),
        name="gather",
    )(inputs, weight, log_decay, out_gain)


def scatter_kernel(line, tiles, out, send_sem, recv_sem, local_sem):
    dp, seq, y, x, z, c = place()
    rows, cols = tiles.shape[2], tiles.shape[3]

    def device(xx, zz, cc):
        return {"dp": 2 * y + xx, "seq": 2 * zz + cc}

    barrier = pltpu.get_barrier_semaphore()
    for zz in range(line):
        for cc in (0, 1):
            @pl.when((zz != z) | (cc != c) | (c != x))
            def _():
                pl.semaphore_signal(
                    barrier, inc=1, device_id=device(c, zz, cc), device_id_type=MESH
                )
    pl.semaphore_wait(barrier, 2 * line - (c == x).astype(jnp.int32))

    def area(zz, cc):
        return out.at[
            pl.ds(pl.multiple_of(cc * rows, rows), rows),
            pl.ds(pl.multiple_of(zz * cols, 128), cols),
        ]

    def push(zz, xx):
        return pltpu.make_async_remote_copy(
            src_ref=tiles.at[zz, xx], dst_ref=area(z, c),
            send_sem=send_sem.at[zz, xx], recv_sem=recv_sem.at[z, c],
            device_id=device(xx, zz, x), device_id_type=MESH,
        )

    def pull(zz, cc):
        return pltpu.make_async_remote_copy(
            src_ref=tiles.at[0, 0], dst_ref=area(zz, cc),
            send_sem=send_sem.at[0, 0], recv_sem=recv_sem.at[zz, cc],
            device_id=device(1 - x, z, c), device_id_type=MESH,
        )

    local = pltpu.make_async_copy(tiles.at[z, x], area(z, c), local_sem)
    own = c == x
    for zz in range(line):
        for xx in (0, 1):
            @pl.when((zz != z) | (xx != x) | jnp.logical_not(own))
            def _():
                push(zz, xx).start()

    @pl.when(own)
    def _():
        local.start()
    for zz in range(line):
        for cc in (0, 1):
            @pl.when((zz != z) | (cc != c) | jnp.logical_not(own))
            def _():
                pull(zz, cc).wait_recv()
    for zz in range(line):
        for xx in (0, 1):
            @pl.when((zz != z) | (xx != x) | jnp.logical_not(own))
            def _():
                push(zz, xx).wait_send()

    @pl.when(own)
    def _():
        local.wait()


def scatter(line, tiles):
    dma = pltpu.SemaphoreType.DMA
    _, _, rows, cols = tiles.shape
    any_space = pl.BlockSpec(memory_space=pl.ANY)
    return pl.pallas_call(
        functools.partial(scatter_kernel, line),
        out_shape=jax.ShapeDtypeStruct((2 * rows, line * cols), tiles.dtype),
        in_specs=[any_space],
        out_specs=any_space,
        scratch_shapes=[dma((line, 2)), dma((line, 2)), dma],
        compiler_params=pltpu.CompilerParams(
            collective_id=1, has_side_effects=True, vmem_limit_bytes=1 << 20
        ),
        name="scatter",
    )(tiles)


def shards_quarter(inputs, qkv_weight, log_decay, out_gain):
    dps, seqs = lax.axis_size("dp"), lax.axis_size("seq")
    dp, seq, y, x, z, c = place()
    line = seqs // 2
    tok = inputs.shape[0]
    chunk = tok // 2
    local_heads, head_size = out_gain.shape
    heads = 4
    grouped, decays, gains = gather(line, inputs, qkv_weight, log_decay, out_gain)
    decays = lax.dynamic_slice_in_dim(decays, 2 * z, 2, axis=2)
    decays = jnp.transpose(decays, (1, 0, 2, 3)).reshape(line, 2, 2, 2, 2, chunk)
    decays = jnp.transpose(decays, (0, 1, 4, 2, 3, 5)).reshape(line, 2, 2, heads, chunk)
    gains = lax.dynamic_slice_in_dim(gains, 2 * z, 2, axis=1).reshape(heads, head_size)
    totals = jnp.sum(decays, axis=-1)
    mine = lax.dynamic_index_in_dim(decays, x, 1, keepdims=False)
    mine = lax.dynamic_index_in_dim(mine, c, 1, keepdims=False)

    grouped = grouped.reshape(3, line * heads, chunk, head_size)
    cumulated = running(mine.reshape(line * heads, chunk))
    intra_term, update, _, queries_decayed = block_terms(
        grouped[0], grouped[1], grouped[2], cumulated
    )
    update = update.reshape(line, heads, head_size, head_size)
    flat = [(d, s) for d in range(dps) for s in range(seqs)]
    core_pairs = [(d * seqs + s, d * seqs + (s ^ 1)) for d, s in flat]
    x_pairs = [(d * seqs + s, (d ^ 1) * seqs + s) for d, s in flat]
    other = lax.ppermute(update, ("dp", "seq"), core_pairs)
    lower = jnp.where(c == 0, update, other)
    upper = jnp.where(c == 0, other, update)
    my_totals = lax.dynamic_index_in_dim(totals, x, 1, keepdims=False)
    joined = jnp.exp(my_totals[:, 1])[..., None, None] * lower + upper
    part = lax.dynamic_slice_in_dim(joined, 2 * c, 2, axis=1)
    part = lax.ppermute(part, ("dp", "seq"), x_pairs)
    part_other = lax.ppermute(part, ("dp", "seq"), core_pairs)
    across = jnp.concatenate(
        [jnp.where(c == 0, part, part_other), jnp.where(c == 0, part_other, part)], axis=1
    )
    state = jnp.zeros_like(update[0])
    block_totals = totals[:, :, 0] + totals[:, :, 1]
    carried = []
    for zz in range(line):
        starts = []
        for xx in (0, 1):
            starts.append(state)
            term = jnp.where(x == xx, joined[zz], across[zz])
            state = jnp.exp(block_totals[zz, xx])[:, None, None] * state + term
        start = jnp.where(x == 0, starts[0], starts[1])
        later = jnp.exp(my_totals[zz, 0])[:, None, None] * start + lower[zz]
        carried.append(jnp.where(c == 0, start, later))
    carried = jnp.concatenate(carried, axis=0)
    normed = finish_heads(intra_term, queries_decayed, carried, jnp.tile(gains, (line, 1)))
    tiles = normed.astype(jnp.bfloat16).reshape(line, 2, 2, chunk, head_size)
    tiles = jnp.transpose(tiles, (0, 1, 3, 2, 4)).reshape(line, 2, chunk, 2 * head_size)
    return scatter(line, tiles)


def solution(mesh):
    in_specs = (P("seq", None), P(None, ("dp", "seq")), P("dp", "seq"), P("dp", None))
    out_specs = P("seq", "dp")

    def shards(inputs, qkv_weight, log_decay, out_gain):
        local_heads, head_size = out_gain.shape
        whole_heads = qkv_weight.shape[1] == 3 * head_size
        fits = whole_heads and local_heads == mesh.shape["seq"] and mesh.shape["dp"] == 4
        body = shards_quarter if fits else shards_wide
        return body(inputs, qkv_weight, log_decay, out_gain)

    return jax.shard_map(shards, mesh=mesh, in_specs=in_specs, out_specs=out_specs, check_vma=False)
```
